32 devices in a mesh: fsdp: 8 (over z, y), tp: 4 (over x, core).
Axes of the slice: x: 2, y: 2, z: 4, core: 2. Of those that a mesh axis runs over, the one named last changes fastest.
Arguments:
- hidden_in: bfloat16 [8, 4, 256, 1152], P('fsdp', 'tp'), may hold values from -6 to 6
- cotangent: bfloat16 [8, 4, 256, 1152], P('fsdp', 'tp'), may hold values from -6 to 6
- image_group: int32 [12], replicated, may hold values from 0 to 7, never falling along the last dimension, each value on 1 to 2 neighbouring positions
- block_sizes: int32 [8, 4], P('fsdp'), may hold values from 1 to 256, 512 in all within a row
- joint_weight: bfloat16 [3, 1152, 1152], P(None, 'fsdp', 'tp'), may hold values from -0.25 to 0.25
- joint_bias: bfloat16 [2, 1152], P(None, 'tp'), may hold values from -3 to 3
- out_weight: bfloat16 [1152, 1152], P('tp', 'fsdp'), may hold values from -0.75 to 0.75
- out_bias: bfloat16 [1152], replicated, may hold values from -2 to 2
- first_gain: bfloat16 [1152], replicated, may hold values from 0.099609375 to 1.8984375
- first_shift: bfloat16 [1152], replicated, may hold values from -2 to 2
- second_gain: bfloat16 [1152], replicated, may hold values from 0.099609375 to 1.8984375
- second_shift: bfloat16 [1152], replicated, may hold values from -2 to 2
- up_weight: bfloat16 [4304, 1152], P('tp', 'fsdp'), may hold values from -0.1875 to 0.1875
- up_bias: bfloat16 [4304], P('tp'), may hold values from -3 to 3
- down_weight: bfloat16 [4304, 1152], P('tp', 'fsdp'), may hold values from -0.09375 to 0.09375
- down_bias: bfloat16 [1152], replicated, may hold values from -2 to 2
Outputs:
- layer_out: bfloat16 [8, 4, 256, 1152], P('fsdp', 'tp')
- input_grad: float32 [8, 4, 256, 1152], P('fsdp', 'tp')
- joint_grad: float32 [3, 1152, 1152], P(None, 'fsdp', 'tp')
- queryvalue_grad: float32 [2, 1152], replicated
- outweight_grad: float32 [1152, 1152], P('tp', 'fsdp')
- outbias_grad: float32 [1152], replicated
- firstgain_grad: float32 [1152], replicated
- firstshift_grad: float32 [1152], replicated
- secondgain_grad: float32 [1152], replicated
- secondshift_grad: float32 [1152], replicated
- upweight_grad: float32 [4304, 1152], P('tp', 'fsdp')
- upbias_grad: float32 [4304], replicated
- downweight_grad: float32 [4304, 1152], P('tp', 'fsdp')
- downbias_grad: float32 [1152], replicated
The draws below stay inside these ranges and needn't reach their ends.
Inputs may be any that keep to these rules, and one draw needn't show every extreme that they name: `image_group`: never falling; every group of fsdp holds 1 to 2 images, some group exactly 2; a group's images fill its slots from the first on. `block_sizes`: each row sums to 512; in each row one device's block holds exactly 256 live rows.
All inputs are finite; a program needn't handle non-finite values.
Results may differ from the reference program's by a relative error of at most 0.012.
The reference program's roundings to bfloat16 on the way count: a program that leaves them out, or rounds other values in their place, can miss the bound.
Values may be sent and summed in bfloat16 or wider, within the bound.
A program may use at most 128 MiB of HBM per device.

```python
import math
import jax
import jax.numpy as jnp
import numpy as np
from jax import lax

D = 1152
H = 16
HD = 72
FF = 4304
SEQ = 256
SLOTS = 2
BLK = 256
IMAGES = 12
N_FSDP = 8
N_TP = 4


def shard_levels(key, dims, split, least, high):
    level, own = 1.0, jax.random.fold_in(key, 6)
    for position, shards_of in split:
        draws = jnp.exp(jax.random.uniform(jax.random.fold_in(own, position), (shards_of,), jnp.float32, least / len(split), high / len(split)))
        level = level * jnp.repeat(draws, dims[position] // shards_of).reshape([-1 if axis == position else 1 for axis in range(len(dims))])
    return level


def profile(amount, total, most, lean):
    portions = [(1 << 20) // math.isqrt(rank ** lean) + 1 for rank in range(2, amount + 1)]
    rest, given = total - most - (amount - 1), [1] * (amount - 1)
    while rest > 0:
        candidates = [i for i in range(amount - 1) if given[i] < most]
        whole, left = sum([portions[i] for i in candidates]), rest
        for i in candidates:
            extra = min(most - given[i], max(1, left * portions[i] // whole), rest)
            given[i] = given[i] + extra
            rest = rest - extra
    return np.array([most] + given)


def ragged(rng, count, total, reach, lean):
    if count == 2:
        one = jax.random.randint(rng, (), max(1, total - reach), min(reach, total - 1) + 1)
        return jnp.stack([one, total - one])
    sizes = jnp.asarray(profile(count, total, reach, lean), jnp.int32)
    couples = (count - 1) // 2
    source_of, receiver = sizes[1:1 + 2 * couples:2], sizes[2:2 + 2 * couples:2]
    margin = jnp.minimum(source_of - 1, reach - receiver)
    passed = jax.random.randint(jax.random.fold_in(rng, 1), (couples,), 0, 1 << 20) % (margin + 1)
    sizes = sizes.at[1:1 + 2 * couples:2].set(source_of - passed).at[2:2 + 2 * couples:2].set(receiver + passed)
    return sizes[jax.random.permutation(jax.random.fold_in(rng, 2), count)]


def noise(stream_key, shape, deviation, bound, split=(), kind=jnp.bfloat16):
    values = jax.random.normal(stream_key, shape, jnp.float32) * deviation
    if len(split) > 0:
        values = shard_levels(stream_key, shape, split, -0.22, 0.18) * values
    return jnp.clip(values, min=-bound, max=bound).astype(kind)


def setup_inputs(seed: int = 0) -> dict:
    key_of = jax.random.split(jax.random.key(seed), 17)
    hidden_in = noise(key_of[0], (N_FSDP, N_TP, BLK, D), 1.0, 6.0, ((0, 8), (1, 4)))
    cotangent = noise(key_of[1], (N_FSDP, N_TP, BLK, D), 1.0, 6.0, ((0, 8), (1, 4)))
    image_group = jnp.searchsorted(jnp.cumsum(ragged(key_of[2], N_FSDP, IMAGES, SLOTS, 0)), jnp.arange(IMAGES), side="right").astype(jnp.int32)
    block_sizes = jax.vmap(lambda own: ragged(own, N_TP, SLOTS * SEQ, BLK, 2))(jax.random.split(key_of[3], N_FSDP)).reshape((N_FSDP, N_TP)).astype(jnp.int32)
    joint_weight = noise(key_of[4], (3, D, D), (D // 2) ** -0.5, 0.25, ((1, 8), (2, 4)))
    joint_bias = noise(key_of[5], (2, D), 0.5, 3.0, ((1, 4),))
    out_weight = noise(key_of[6], (D, D), (D // 16) ** -0.5, 0.75, ((0, 4), (1, 8)))
    out_bias = noise(key_of[7], (D,), 0.3, 2.0)
    first_gain = jnp.clip(1.0 + 0.18 * jax.random.normal(key_of[8], (D,), jnp.float32), 0.099609375, 1.8984375).astype(jnp.bfloat16)
    first_shift = noise(key_of[9], (D,), 0.3, 2.0)
    second_gain = jnp.clip(1.0 + 0.18 * jax.random.normal(key_of[10], (D,), jnp.float32), 0.099609375, 1.8984375).astype(jnp.bfloat16)
    second_shift = noise(key_of[11], (D,), 0.3, 2.0)
    up_weight = noise(key_of[12], (FF, D), D ** -0.5, 0.1875, ((0, 4), (1, 8)))
    up_bias = noise(key_of[13], (FF,), 0.5, 3.0, ((0, 4),))
    down_weight = noise(key_of[14], (FF, D), FF ** -0.5, 0.09375, ((0, 4), (1, 8)))
    down_bias = noise(key_of[15], (D,), 0.3, 2.0)
    return {"hidden_in": hidden_in, "cotangent": cotangent, "image_group": image_group, "block_sizes": block_sizes, "joint_weight": joint_weight, "joint_bias": joint_bias, "out_weight": out_weight, "out_bias": out_bias, "first_gain": first_gain, "first_shift": first_shift, "second_gain": second_gain, "second_shift": second_shift, "up_weight": up_weight, "up_bias": up_bias, "down_weight": down_weight, "down_bias": down_bias}


EPSILON = 1e-06
HIGHEST = lax.Precision.HIGHEST

@jax.custom_vjp
def low(v):
    return lax.optimization_barrier(v.astype(jnp.bfloat16)).astype(jnp.float32)

@jax.custom_vjp
def low_back(v):
    return v

def low_keep(v):
    return (low(v), None)

def low_pass(kept, grad):
    return (grad,)

def back_keep(v):
    return (v, None)

def back_low(kept, grad):
    return (low(grad),)
low.defvjp(low_keep, low_pass)
low_back.defvjp(back_keep, back_low)

def matmul(former, latter):
    return jnp.dot(former, latter, precision=HIGHEST)

def layer_norm(values, scale_row, shift_row):
    center = values - lax.optimization_barrier(jnp.mean(values, axis=-1, keepdims=True))
    spread = lax.optimization_barrier(jnp.mean(center * center, axis=-1, keepdims=True))
    return center * lax.rsqrt(spread + EPSILON) * scale_row + shift_row

def gelu_tanh(values):
    return 0.5 * values * (1.0 + jnp.tanh(0.7978845608028654 * (values + 0.044715 * values * values * values)))

def forward_layer(tokens, live, joint_weight, joint_bias, out_weight, out_bias, first_gain, first_shift, second_gain, second_shift, up_weight, up_bias, down_weight, down_bias):
    score_scale = 1.0 / math.sqrt(HD)
    slot_rows = SLOTS * SEQ
    normed_one = low(layer_norm(tokens, first_gain, first_shift))
    query_rows = low(low_back(matmul(normed_one, joint_weight[0]) + joint_bias[0]))
    key_rows = low(low_back(matmul(normed_one, joint_weight[1])))
    value_rows = low(low_back(matmul(normed_one, joint_weight[2]) + joint_bias[1]))
    head_shape = (SLOTS, SEQ, H, HD)
    scores = low_back(jnp.einsum('aqhd,akhd->ahqk', query_rows.reshape(head_shape), key_rows.reshape(head_shape), precision=HIGHEST) * score_scale)
    probs_full = jax.nn.softmax(scores, axis=-1)
    mixed = jnp.einsum('ahqk,akhd->aqhd', low(probs_full), value_rows.reshape(head_shape), precision=HIGHEST)
    mixed_rows = low(low_back(mixed.reshape(slot_rows, D)))
    residual = tokens + low_back(matmul(mixed_rows, out_weight)) + out_bias
    normed_two = low(layer_norm(residual, second_gain, second_shift))
    preact = low_back(jnp.dot(normed_two, up_weight.T, precision=HIGHEST) + up_bias)
    activated = low(gelu_tanh(preact))
    layer_sum = residual + low_back(matmul(activated, down_weight)) + down_bias
    return layer_sum * live[:, None]

def reference(hidden_in, cotangent, image_group, block_sizes, joint_weight, joint_bias, out_weight, out_bias, first_gain, first_shift, second_gain, second_shift, up_weight, up_bias, down_weight, down_bias):
    params = tuple((arr.astype(jnp.float32) for arr in (joint_weight, joint_bias, out_weight, out_bias, first_gain, first_shift, second_gain, second_shift, up_weight, up_bias, down_weight, down_bias)))
    slot_rows = SLOTS * SEQ
    slot_index = jnp.arange(slot_rows, dtype=jnp.int32)
    group_numbers = jnp.arange(N_FSDP, dtype=jnp.int32)
    image_counts = lax.optimization_barrier(jnp.sum((image_group[None, :] == group_numbers[:, None]).astype(jnp.int32), axis=1))

    def one_group(totals, group_item):
        tokens_group, cotangent_group, block_row, image_count = group_item
        starts = jnp.cumsum(block_row) - block_row
        owner_block = lax.optimization_barrier(jnp.sum((slot_index[:, None] >= starts[None, 1:]).astype(jnp.int32), axis=1))
        flat_index = (owner_block * BLK + slot_index - starts[owner_block]).astype(jnp.int32)
        tokens = tokens_group.reshape(N_TP * BLK, D)[flat_index].astype(jnp.float32)
        seeds = cotangent_group.reshape(N_TP * BLK, D)[flat_index].astype(jnp.float32)
        live = (slot_index // SEQ < image_count).astype(jnp.float32)

        def run_layer(tokens_value, *weights):
            return forward_layer(tokens_value, live, *weights)
        result, pull = jax.vjp(run_layer, tokens, *params)
        grads = pull(seeds)
        out_buffer = jnp.zeros((N_TP * BLK, D), jnp.float32).at[flat_index].set(result)
        grad_buffer = jnp.zeros((N_TP * BLK, D), jnp.float32).at[flat_index].set(grads[0])
        totals = tuple((first + second for first, second in zip(totals, grads[1:])))
        return (totals, (out_buffer.astype(jnp.bfloat16).reshape(N_TP, BLK, D), grad_buffer.reshape(N_TP, BLK, D)))
    initial = tuple((jnp.zeros(arr.shape, jnp.float32) for arr in params))
    totals, stacked = lax.scan(one_group, initial, (hidden_in, cotangent, block_sizes, image_counts))
    return (stacked[0], stacked[1], totals[0], totals[1], totals[2], totals[3], totals[4], totals[5], totals[6], totals[7], totals[8], totals[9], totals[10], totals[11])
```

```python
import math

import jax
import jax.numpy as jnp
from jax import lax
from jax.sharding import PartitionSpec as P

HD = 72
SEQ = 256
SLOTS = 2


EPSILON = 1e-06


def layer_norm(values, scale_row, shift_row):
    center = values - jnp.mean(values, axis=-1, keepdims=True)
    spread = jnp.mean(center * center, axis=-1, keepdims=True)
    return center * lax.rsqrt(spread + EPSILON) * scale_row + shift_row


def gelu_tanh(values):
    return (
        0.5
        * values
        * (1.0 + jnp.tanh(0.7978845608028654 * (values + 0.044715 * values * values * values)))
    )


def contract(former, latter, former_dim, latter_dim):
    return lax.dot_general(
        former,
        latter,
        (((former_dim,), (latter_dim,)), ((), ())),
        preferred_element_type=jnp.float32,
    )


def local(
    hidden_in,
    cotangent,
    image_group,
    block_sizes,
    joint_weight,
    joint_bias,
    out_weight,
    out_bias,
    first_gain,
    first_shift,
    second_gain,
    second_shift,
    up_weight,
    up_bias,
    down_weight,
    down_bias,
):
    split_count = lax.axis_size("tp")
    split_index = lax.axis_index("tp")
    group_index = lax.axis_index("fsdp")
    buffer_rows = hidden_in.shape[2]
    width = hidden_in.shape[3]
    slot_rows = SLOTS * SEQ
    local_width = joint_weight.shape[2]
    local_heads = local_width // HD
    hidden_local = up_weight.shape[0]
    score_scale = 1.0 / math.sqrt(HD)
    half = slot_rows // 2
    core = split_index % 2
    low = jnp.bfloat16
    f32 = jnp.float32
    sibling = [(i, i ^ 1) for i in range(split_count)]
    across = [(i, i ^ 2) for i in range(split_count)]

    groups = lax.axis_size("fsdp")
    ringed = groups == 8
    ring = list(range(groups))
    if ringed:
        ring = ring[0::2] + ring[1::2][::-1]
    forth = [(ring[i], ring[(i + 1) % groups]) for i in range(groups)]
    back = [(b, a) for a, b in forth]
    depth = joint_weight.shape[1]
    cut = (depth // 32) * 16
    places = jnp.array(ring, jnp.int32)
    position = jnp.sum(jnp.where(places == group_index, jnp.arange(groups), 0))
    feature = jnp.arange(width, dtype=jnp.int32)
    near_index = (position + feature // depth) % groups
    if not ringed:
        near_index = feature // depth
    owner = jnp.sum(
        jnp.where(near_index[:, None] == jnp.arange(groups)[None, :], places[None, :], 0), axis=1
    )
    source = owner * depth + feature % depth
    turn = (feature[:, None] == source[None, :]).astype(low)

    def ring_gather(shard):
        if not ringed:
            return lax.all_gather(shard, "fsdp", axis=0, tiled=True)
        ahead, behind = [], []
        first = second = shard
        for _ in range(groups // 2 - 1):
            first = lax.ppermute(first, "fsdp", forth)
            second = lax.ppermute(second, "fsdp", back)
            behind.append(first)
            ahead.append(second)
        top = lax.ppermute(first[:cut], "fsdp", forth)
        bottom = lax.ppermute(second[cut:], "fsdp", back)
        mixed = jnp.concatenate([shard, *ahead, top, bottom, *behind[::-1]], axis=0)
        return jnp.dot(turn, mixed, preferred_element_type=f32).astype(low)

    def ring_order(values):
        if not ringed:
            return values
        return jnp.dot(values, turn, preferred_element_type=f32).astype(low)

    def ring_scatter(terms):
        if not ringed:
            return lax.psum_scatter(
                terms.astype(low), "fsdp", scatter_dimension=0, tiled=True
            ).astype(f32)
        middle = groups // 2

        def chunk(number):
            return terms[number * depth : (number + 1) * depth]

        far = chunk(middle).astype(low)
        top = lax.ppermute(far[:cut], "fsdp", forth).astype(f32)
        bottom = lax.ppermute(far[cut:], "fsdp", back).astype(f32)
        held = chunk(middle - 1)
        first = jnp.concatenate([held[:cut] + top, held[cut:]], axis=0)
        held = chunk(middle + 1)
        second = jnp.concatenate([held[:cut], held[cut:] + bottom], axis=0)
        for step in range(1, middle):
            first = lax.ppermute(first.astype(low), "fsdp", forth).astype(f32)
            second = lax.ppermute(second.astype(low), "fsdp", back).astype(f32)
            if step < middle - 1:
                first = first + chunk(middle - 1 - step)
                second = second + chunk(middle + 1 + step)
        return chunk(0) + first + second

    def sum_everywhere(values):
        for axis in ("tp", "fsdp"):
            size, bit = lax.axis_size(axis), 1
            while bit < size:
                pairs = [(i, i ^ bit) for i in range(size)]
                values = values + lax.ppermute(values, axis, pairs)
                bit *= 2
        return values

    def join(mine, other, side):
        first = side == 0
        return jnp.concatenate([jnp.where(first, mine, other), jnp.where(first, other, mine)], 0)

    def gather_blocks(block):
        far = lax.ppermute(block, "tp", across)
        pair = join(block, far, split_index // 2)
        other = lax.ppermute(pair, "tp", sibling)
        mine = pair.reshape(2, buffer_rows, width)
        theirs = other.reshape(2, buffer_rows, width)
        first = core == 0
        return jnp.stack(
            [jnp.where(first, mine, theirs), jnp.where(first, theirs, mine)], 1
        ).reshape(split_count * buffer_rows, width)

    def sum_slots(partial):
        kept = lax.dynamic_slice_in_dim(partial, core * half, half, 0)
        given = lax.dynamic_slice_in_dim(partial, (1 - core) * half, half, 0)
        near = lax.ppermute(given.astype(low), "tp", sibling)
        chip = (kept + near.astype(f32)).astype(low)
        far = lax.ppermute(chip, "tp", across)
        whole = (chip.astype(f32) + far.astype(f32)).astype(low)
        other = lax.ppermute(whole, "tp", sibling)
        return join(whole, other, core)

    block_lengths = block_sizes[0]
    starts = jnp.cumsum(block_lengths) - block_lengths
    block_numbers = jnp.arange(split_count, dtype=jnp.int32)
    slot_index = jnp.arange(slot_rows, dtype=jnp.int32)
    owner_block = jnp.sum((slot_index[:, None] >= starts[None, 1:]).astype(jnp.int32), axis=1)
    owner_start = jnp.sum(
        jnp.where(owner_block[:, None] == block_numbers[None, :], starts[None, :], 0), axis=1
    )
    flat_index = owner_block * buffer_rows + slot_index - owner_start
    place = (
        flat_index[:, None] == jnp.arange(split_count * buffer_rows, dtype=jnp.int32)[None, :]
    ).astype(low)
    image_count = jnp.sum((image_group == group_index).astype(jnp.int32))
    live = (slot_index // SEQ < image_count).astype(f32)[:, None]
    own_start = jnp.sum(jnp.where(block_numbers == split_index, starts, 0))
    own_length = jnp.sum(jnp.where(block_numbers == split_index, block_lengths, 0))
    offsets = jnp.arange(buffer_rows, dtype=jnp.int32)
    own_used = offsets < own_length
    own_slot = own_start + offsets
    pick = ((own_slot[:, None] == slot_index[None, :]) & own_used[:, None]).astype(low)
    own_live = (own_used & (own_slot // SEQ < image_count)).astype(f32)[:, None]

    def to_slots(gathered):
        return jnp.dot(place, gathered, preferred_element_type=f32)

    def own_rows(values):
        return jnp.dot(pick, values, preferred_element_type=f32)

    def split_heads(values):
        return values.reshape(SLOTS, SEQ, local_heads, HD)

    gain_early = first_gain.astype(f32)
    shift_early = first_shift.astype(f32)
    gain_late = second_gain.astype(f32)
    shift_late = second_shift.astype(f32)
    attention_shard = jnp.concatenate(
        [joint_weight[0], joint_weight[1], joint_weight[2], out_weight.T], axis=1
    )
    attention_full = ring_gather(attention_shard)
    up_full = lax.all_gather(up_weight.T, "fsdp", axis=0, tiled=True)
    down_full = lax.all_gather(down_weight.T, "fsdp", axis=0, tiled=True)
    joint_full = attention_full[:, : 3 * local_width]
    out_full = attention_full[:, 3 * local_width :]

    tokens = to_slots(gather_blocks(hidden_in[0, 0]))
    attention_rows = layer_norm(tokens, gain_early, shift_early).astype(low)
    bias_row = jnp.concatenate(
        [
            joint_bias[0].astype(f32),
            jnp.zeros((local_width,), f32),
            joint_bias[1].astype(f32),
        ]
    )
    projected = (jnp.dot(attention_rows, joint_full, preferred_element_type=f32) + bias_row).astype(
        low
    )
    query_heads = split_heads(projected[:, :local_width])
    key_heads = split_heads(projected[:, local_width : 2 * local_width])
    value_heads = split_heads(projected[:, 2 * local_width :])
    scores = (
        jnp.einsum("aqhd,akhd->ahqk", query_heads, key_heads, preferred_element_type=f32)
        * score_scale
    )
    raised = jnp.exp(scores - jnp.max(scores, axis=-1, keepdims=True))
    probs = raised * (1.0 / jnp.sum(raised, axis=-1, keepdims=True))
    weights_low = probs.astype(low)
    mixed_rows = jnp.einsum("ahqk,akhd->aqhd", weights_low, value_heads, preferred_element_type=f32)
    mixed_rows = mixed_rows.reshape(slot_rows, local_width).astype(low)
    mixed_sum = sum_slots(contract(mixed_rows, out_full, 1, 1))
    out_shift = out_bias.astype(f32)
    residual = tokens + mixed_sum.astype(f32) + out_shift
    feed_input = layer_norm(residual, gain_late, shift_late).astype(low)

    output_rows = to_slots(gather_blocks(cotangent[0, 0])) * live
    output_low = output_rows.astype(low)

    preact = jnp.dot(feed_input, up_full, preferred_element_type=f32) + up_bias.astype(f32)
    activated = gelu_tanh(preact).astype(low)
    grad_act = jnp.dot(output_low, down_full, preferred_element_type=f32)
    grad_pre = jax.vjp(gelu_tanh, preact)[1](grad_act)[0].astype(low)
    grad_two = sum_slots(contract(grad_pre, up_full, 1, 1)).astype(f32)
    down_grad = contract(output_low, activated, 0, 0).astype(low)
    down_shard = lax.psum_scatter(down_grad, "fsdp", scatter_dimension=0, tiled=True)
    up_grad = contract(feed_input, grad_pre, 0, 0).astype(low)
    up_shard = lax.psum_scatter(up_grad, "fsdp", scatter_dimension=0, tiled=True)
    feed_sum = sum_slots(contract(activated, down_full, 1, 1))
    own_residual = hidden_in[0, 0].astype(f32) + own_rows(mixed_sum) + out_shift
    layer_sum = own_residual + own_rows(feed_sum) + down_bias.astype(f32)
    layer_out = (layer_sum * own_live).astype(low)[None, None]

    late_back = jax.vjp(layer_norm, residual, gain_late, shift_late)[1](grad_two)
    grad_residual = output_rows + late_back[0]
    residual_low = grad_residual.astype(low)
    grad_mixed = jnp.dot(residual_low, out_full, preferred_element_type=f32).astype(low)
    out_grad = contract(ring_order(residual_low), mixed_rows, 0, 0)
    grad_heads = split_heads(grad_mixed)
    grad_probs = jnp.einsum("aqhd,akhd->ahqk", grad_heads, value_heads, preferred_element_type=f32)
    grad_value = jnp.einsum(
        "ahqk,aqhd->akhd", weights_low, grad_heads, preferred_element_type=f32
    ).astype(low)
    inner_sum = jnp.sum(probs * grad_probs, axis=-1, keepdims=True)
    grad_scores = (probs * (grad_probs - inner_sum)).astype(low)
    grad_query = (
        jnp.einsum("ahqk,akhd->aqhd", grad_scores, key_heads, preferred_element_type=f32)
        * score_scale
    ).astype(low)
    grad_key = (
        jnp.einsum("ahqk,aqhd->akhd", grad_scores, query_heads, preferred_element_type=f32)
        * score_scale
    ).astype(low)
    grad_joint = jnp.concatenate(
        [
            grad_query.reshape(slot_rows, local_width),
            grad_key.reshape(slot_rows, local_width),
            grad_value.reshape(slot_rows, local_width),
        ],
        axis=1,
    )
    grad_one = sum_slots(contract(grad_joint, joint_full, 1, 1))
    joint_grad = contract(ring_order(attention_rows), grad_joint, 0, 0)
    attention_grad = jnp.concatenate([joint_grad, out_grad], axis=1)
    attention_part = ring_scatter(attention_grad)
    residual_rest = (grad_residual - residual_low.astype(f32)).astype(low)
    own_grad = own_rows(residual_low) + own_rows(residual_rest)
    early_back = jax.vjp(layer_norm, hidden_in[0, 0].astype(f32), gain_early, shift_early)[1](
        own_rows(grad_one)
    )
    input_grad = (own_grad + early_back[0])[None, None]
    joint_shard = jnp.stack(
        [attention_part[:, i * local_width : (i + 1) * local_width] for i in range(3)]
    )
    out_shard = attention_part[:, 3 * local_width :].T

    def one_of(values):
        return jnp.where(split_index == 0, values, 0.0)

    joint_sums = jnp.sum(grad_joint.astype(f32), axis=0)
    bias_whole = lax.dynamic_update_slice_in_dim(
        jnp.zeros((2, local_width * split_count), f32),
        jnp.stack([joint_sums[:local_width], joint_sums[2 * local_width :]]),
        split_index * local_width,
        1,
    )
    upbias_whole = lax.dynamic_update_slice_in_dim(
        jnp.zeros((hidden_local * split_count,), f32),
        jnp.sum(grad_pre.astype(f32), axis=0),
        split_index * hidden_local,
        0,
    )
    pieces = [
        bias_whole.reshape(-1),
        one_of(jnp.sum(grad_residual, axis=0)),
        early_back[1],
        early_back[2],
        one_of(late_back[1]),
        one_of(late_back[2]),
        upbias_whole,
        one_of(jnp.sum(output_rows, axis=0)),
    ]
    summed = sum_everywhere(jnp.concatenate(pieces))
    small_sums, at = [], 0
    for piece in pieces:
        small_sums.append(lax.slice_in_dim(summed, at, at + piece.shape[0]))
        at += piece.shape[0]
    return (
        layer_out,
        input_grad,
        joint_shard,
        small_sums[0].reshape(2, width),
        out_shard,
        small_sums[1],
        small_sums[2],
        small_sums[3],
        small_sums[4],
        small_sums[5],
        up_shard.astype(f32).T,
        small_sums[6],
        down_shard.astype(f32).T,
        small_sums[7],
    )


def solution(mesh):
    placed = (
        P("fsdp", "tp", None, None),
        P("fsdp", "tp", None, None),
        P(),
        P("fsdp", None),
        P(None, "fsdp", "tp"),
        P(None, "tp"),
        P("tp", "fsdp"),
        P(),
        P(),
        P(),
        P(),
        P(),
        P("tp", "fsdp"),
        P("tp"),
        P("tp", "fsdp"),
        P(),
    )
    return jax.shard_map(
        local,
        mesh=mesh,
        in_specs=placed,
        out_specs=(
            P("fsdp", "tp", None, None),
            P("fsdp", "tp", None, None),
            P(None, "fsdp", "tp"),
            P(),
            P("tp", "fsdp"),
            P(),
            P(),
            P(),
            P(),
            P(),
            P("tp", "fsdp"),
            P(),
            P("tp", "fsdp"),
            P(),
        ),
        check_vma=False,
    )
```

```python
import math

import jax
import jax.numpy as jnp
from jax import lax
from jax.sharding import PartitionSpec as P

HD = 72
SEQ = 256
SLOTS = 2


EPSILON = 1e-06


def layer_norm(values, scale_row, shift_row):
    center = values - jnp.mean(values, axis=-1, keepdims=True)
    spread = jnp.mean(center * center, axis=-1, keepdims=True)
    return center * lax.rsqrt(spread + EPSILON) * scale_row + shift_row


def gelu_tanh(values):
    return (
        0.5
        * values
        * (1.0 + jnp.tanh(0.7978845608028654 * (values + 0.044715 * values * values * values)))
    )


def contract(former, latter, former_dim, latter_dim):
    return lax.dot_general(
        former,
        latter,
        (((former_dim,), (latter_dim,)), ((), ())),
        preferred_element_type=jnp.float32,
    )


def local(
    hidden_in,
    cotangent,
    image_group,
    block_sizes,
    joint_weight,
    joint_bias,
    out_weight,
    out_bias,
    first_gain,
    first_shift,
    second_gain,
    second_shift,
    up_weight,
    up_bias,
    down_weight,
    down_bias,
):
    split_count = lax.axis_size("tp")
    split_index = lax.axis_index("tp")
    group_index = lax.axis_index("fsdp")
    buffer_rows = hidden_in.shape[2]
    width = hidden_in.shape[3]
    slot_rows = SLOTS * SEQ
    local_width = joint_weight.shape[2]
    local_heads = local_width // HD
    hidden_local = up_weight.shape[0]
    score_scale = 1.0 / math.sqrt(HD)
    half = slot_rows // 2
    core = split_index % 2
    low = jnp.bfloat16
    f32 = jnp.float32
    sibling = [(i, i ^ 1) for i in range(split_count)]
    across = [(i, i ^ 2) for i in range(split_count)]

    groups = lax.axis_size("fsdp")
    ringed = groups == 8
    ring = list(range(groups))
    if ringed:
        ring = ring[0::2] + ring[1::2][::-1]
    forth = [(ring[i], ring[(i + 1) % groups]) for i in range(groups)]
    back = [(b, a) for a, b in forth]
    depth = joint_weight.shape[1]
    cut = (depth // 32) * 16
    places = jnp.array(ring, jnp.int32)
    position = jnp.sum(jnp.where(places == group_index, jnp.arange(groups), 0))
    feature = jnp.arange(width, dtype=jnp.int32)
    near_index = (position + feature // depth) % groups
    if not ringed:
        near_index = feature // depth
    owner = jnp.sum(
        jnp.where(near_index[:, None] == jnp.arange(groups)[None, :], places[None, :], 0), axis=1
    )
    source = owner * depth + feature % depth
    turn = (feature[:, None] == source[None, :]).astype(low)

    def ring_gather(shard):
        if not ringed:
            return lax.all_gather(shard, "fsdp", axis=0, tiled=True)
        ahead, behind = [], []
        first = second = shard
        for _ in range(groups // 2 - 1):
            first = lax.ppermute(first, "fsdp", forth)
            second = lax.ppermute(second, "fsdp", back)
            behind.append(first)
            ahead.append(second)
        top = lax.ppermute(first[:cut], "fsdp", forth)
        bottom = lax.ppermute(second[cut:], "fsdp", back)
        mixed = jnp.concatenate([shard, *ahead, top, bottom, *behind[::-1]], axis=0)
        return jnp.dot(turn, mixed, preferred_element_type=f32).astype(low)

    def ring_order(values):
        if not ringed:
            return values
        return jnp.dot(values, turn, preferred_element_type=f32).astype(low)

    def ring_scatter(terms):
        if not ringed:
            return lax.psum_scatter(
                terms.astype(low), "fsdp", scatter_dimension=0, tiled=True
            ).astype(f32)
        middle = groups // 2

        def chunk(number):
            return terms[number * depth : (number + 1) * depth]

        far = chunk(middle).astype(low)
        top = lax.ppermute(far[:cut], "fsdp", forth).astype(f32)
        bottom = lax.ppermute(far[cut:], "fsdp", back).astype(f32)
        held = chunk(middle - 1)
        first = jnp.concatenate([held[:cut] + top, held[cut:]], axis=0)
        held = chunk(middle + 1)
        second = jnp.concatenate([held[:cut], held[cut:] + bottom], axis=0)
        for step in range(1, middle):
            first = lax.ppermute(first.astype(low), "fsdp", forth).astype(f32)
            second = lax.ppermute(second.astype(low), "fsdp", back).astype(f32)
            if step < middle - 1:
                first = first + chunk(middle - 1 - step)
                second = second + chunk(middle + 1 + step)
        return chunk(0) + first + second

    def sum_everywhere(values):
        for axis in ("tp", "fsdp"):
            size, bit = lax.axis_size(axis), 1
            while bit < size:
                pairs = [(i, i ^ bit) for i in range(size)]
                values = values + lax.ppermute(values, axis, pairs)
                bit *= 2
        return values

    def join(mine, other, side):
        first = side == 0
        return jnp.concatenate([jnp.where(first, mine, other), jnp.where(first, other, mine)], 0)

    def gather_blocks(block):
        far = lax.ppermute(block, "tp", across)
        pair = join(block, far, split_index // 2)
        other = lax.ppermute(pair, "tp", sibling)
        mine = pair.reshape(2, buffer_rows, width)
        theirs = other.reshape(2, buffer_rows, width)
        first = core == 0
        return jnp.stack(
            [jnp.where(first, mine, theirs), jnp.where(first, theirs, mine)], 1
        ).reshape(split_count * buffer_rows, width)

    def sum_slots(partial):
        kept = lax.dynamic_slice_in_dim(partial, core * half, half, 0)
        given = lax.dynamic_slice_in_dim(partial, (1 - core) * half, half, 0)
        near = lax.ppermute(given.astype(low), "tp", sibling)
        chip = (kept + near.astype(f32)).astype(low)
        far = lax.ppermute(chip, "tp", across)
        whole = (chip.astype(f32) + far.astype(f32)).astype(low)
        other = lax.ppermute(whole, "tp", sibling)
        return join(whole, other, core)

    block_lengths = block_sizes[0]
    starts = jnp.cumsum(block_lengths) - block_lengths
    block_numbers = jnp.arange(split_count, dtype=jnp.int32)
    slot_index = jnp.arange(slot_rows, dtype=jnp.int32)
    owner_block = jnp.sum((slot_index[:, None] >= starts[None, 1:]).astype(jnp.int32), axis=1)
    owner_start = jnp.sum(
        jnp.where(owner_block[:, None] == block_numbers[None, :], starts[None, :], 0), axis=1
    )
    flat_index = owner_block * buffer_rows + slot_index - owner_start
    place = (
        flat_index[:, None] == jnp.arange(split_count * buffer_rows, dtype=jnp.int32)[None, :]
    ).astype(low)
    image_count = jnp.sum((image_group == group_index).astype(jnp.int32))
    live = (slot_index // SEQ < image_count).astype(f32)[:, None]
    own_start = jnp.sum(jnp.where(block_numbers == split_index, starts, 0))
    own_length = jnp.sum(jnp.where(block_numbers == split_index, block_lengths, 0))
    offsets = jnp.arange(buffer_rows, dtype=jnp.int32)
    own_used = offsets < own_length
    own_slot = own_start + offsets
    pick = ((own_slot[:, None] == slot_index[None, :]) & own_used[:, None]).astype(low)
    own_live = (own_used & (own_slot // SEQ < image_count)).astype(f32)[:, None]

    def to_slots(gathered):
        return jnp.dot(place, gathered, preferred_element_type=f32)

    def own_rows(values):
        return jnp.dot(pick, values, preferred_element_type=f32)

    def split_heads(values):
        return values.reshape(SLOTS, SEQ, local_heads, HD)

    gain_early = first_gain.astype(f32)
    shift_early = first_shift.astype(f32)
    gain_late = second_gain.astype(f32)
    shift_late = second_shift.astype(f32)
    attention_shard = jnp.concatenate(
        [joint_weight[0], joint_weight[1], joint_weight[2], out_weight.T], axis=1
    )
    attention_full = lax.all_gather(attention_shard, "fsdp", axis=0, tiled=True)
    up_full = lax.all_gather(up_weight.T, "fsdp", axis=0, tiled=True)
    down_full = ring_gather(down_weight.T)
    joint_full = attention_full[:, : 3 * local_width]
    out_full = attention_full[:, 3 * local_width :]

    tokens = to_slots(gather_blocks(hidden_in[0, 0]))
    attention_rows = layer_norm(tokens, gain_early, shift_early).astype(low)
    bias_row = jnp.concatenate(
        [
            joint_bias[0].astype(f32),
            jnp.zeros((local_width,), f32),
            joint_bias[1].astype(f32),
        ]
    )
    projected = (jnp.dot(attention_rows, joint_full, preferred_element_type=f32) + bias_row).astype(
        low
    )
    query_heads = split_heads(projected[:, :local_width])
    key_heads = split_heads(projected[:, local_width : 2 * local_width])
    value_heads = split_heads(projected[:, 2 * local_width :])
    scores = (
        jnp.einsum("aqhd,akhd->ahqk", query_heads, key_heads, preferred_element_type=f32)
        * score_scale
    )
    raised = jnp.exp(scores - jnp.max(scores, axis=-1, keepdims=True))
    probs = raised * (1.0 / jnp.sum(raised, axis=-1, keepdims=True))
    weights_low = probs.astype(low)
    mixed_rows = jnp.einsum("ahqk,akhd->aqhd", weights_low, value_heads, preferred_element_type=f32)
    mixed_rows = mixed_rows.reshape(slot_rows, local_width).astype(low)
    mixed_sum = sum_slots(contract(mixed_rows, out_full, 1, 1))
    out_shift = out_bias.astype(f32)
    residual = tokens + mixed_sum.astype(f32) + out_shift
    feed_input = layer_norm(residual, gain_late, shift_late).astype(low)

    output_rows = to_slots(gather_blocks(cotangent[0, 0])) * live
    output_low = output_rows.astype(low)

    preact = jnp.dot(feed_input, up_full, preferred_element_type=f32) + up_bias.astype(f32)
    activated = gelu_tanh(preact).astype(low)
    grad_act = jnp.dot(output_low, down_full, preferred_element_type=f32)
    grad_pre = jax.vjp(gelu_tanh, preact)[1](grad_act)[0].astype(low)
    grad_two = sum_slots(contract(grad_pre, up_full, 1, 1)).astype(f32)
    down_grad = contract(output_low, activated, 0, 0).astype(low)
    down_shard = lax.psum_scatter(down_grad, "fsdp", scatter_dimension=0, tiled=True)
    up_grad = contract(feed_input, grad_pre, 0, 0).astype(low)
    up_shard = lax.psum_scatter(up_grad, "fsdp", scatter_dimension=0, tiled=True)
    feed_sum = sum_slots(contract(activated, down_full, 1, 1))
    own_residual = hidden_in[0, 0].astype(f32) + own_rows(mixed_sum) + out_shift
    layer_sum = own_residual + own_rows(feed_sum) + down_bias.astype(f32)
    layer_out = (layer_sum * own_live).astype(low)[None, None]

    late_back = jax.vjp(layer_norm, residual, gain_late, shift_late)[1](grad_two)
    grad_residual = output_rows + late_back[0]
    residual_low = grad_residual.astype(low)
    grad_mixed = jnp.dot(residual_low, out_full, preferred_element_type=f32).astype(low)
    out_grad = contract(ring_order(residual_low), mixed_rows, 0, 0)
    grad_heads = split_heads(grad_mixed)
    grad_probs = jnp.einsum("aqhd,akhd->ahqk", grad_heads, value_heads, preferred_element_type=f32)
    grad_value = jnp.einsum(
        "ahqk,aqhd->akhd", weights_low, grad_heads, preferred_element_type=f32
    ).astype(low)
    inner_sum = jnp.sum(probs * grad_probs, axis=-1, keepdims=True)
    grad_scores = (probs * (grad_probs - inner_sum)).astype(low)
    grad_query = (
        jnp.einsum("ahqk,akhd->aqhd", grad_scores, key_heads, preferred_element_type=f32)
        * score_scale
    ).astype(low)
    grad_key = (
        jnp.einsum("ahqk,aqhd->akhd", grad_scores, query_heads, preferred_element_type=f32)
        * score_scale
    ).astype(low)
    grad_joint = jnp.concatenate(
        [
            grad_query.reshape(slot_rows, local_width),
            grad_key.reshape(slot_rows, local_width),
            grad_value.reshape(slot_rows, local_width),
        ],
        axis=1,
    )
    grad_one = sum_slots(contract(grad_joint, joint_full, 1, 1))
    joint_grad = contract(ring_order(attention_rows), grad_joint, 0, 0)
    attention_grad = jnp.concatenate([joint_grad, out_grad], axis=1)
    attention_part = ring_scatter(attention_grad)
    residual_rest = (grad_residual - residual_low.astype(f32)).astype(low)
    own_grad = own_rows(residual_low) + own_rows(residual_rest)
    early_back = jax.vjp(layer_norm, hidden_in[0, 0].astype(f32), gain_early, shift_early)[1](
        own_rows(grad_one)
    )
    input_grad = (own_grad + early_back[0])[None, None]
    joint_shard = jnp.stack(
        [attention_part[:, i * local_width : (i + 1) * local_width] for i in range(3)]
    )
    out_shard = attention_part[:, 3 * local_width :].T

    def one_of(values):
        return jnp.where(split_index == 0, values, 0.0)

    joint_sums = jnp.sum(grad_joint.astype(f32), axis=0)
    bias_whole = lax.dynamic_update_slice_in_dim(
        jnp.zeros((2, local_width * split_count), f32),
        jnp.stack([joint_sums[:local_width], joint_sums[2 * local_width :]]),
        split_index * local_width,
        1,
    )
    upbias_whole = lax.dynamic_update_slice_in_dim(
        jnp.zeros((hidden_local * split_count,), f32),
        jnp.sum(grad_pre.astype(f32), axis=0),
        split_index * hidden_local,
        0,
    )
    pieces = [
        bias_whole.reshape(-1),
        one_of(jnp.sum(grad_residual, axis=0)),
        early_back[1],
        early_back[2],
        one_of(late_back[1]),
        one_of(late_back[2]),
        upbias_whole,
        one_of(jnp.sum(output_rows, axis=0)),
    ]
    summed = sum_everywhere(jnp.concatenate(pieces))
    small_sums, at = [], 0
    for piece in pieces:
        small_sums.append(lax.slice_in_dim(summed, at, at + piece.shape[0]))
        at += piece.shape[0]
    return (
        layer_out,
        input_grad,
        joint_shard,
        small_sums[0].reshape(2, width),
        out_shard,
        small_sums[1],
        small_sums[2],
        small_sums[3],
        small_sums[4],
        small_sums[5],
        up_shard.astype(f32).T,
        small_sums[6],
        down_shard.astype(f32).T,
        small_sums[7],
    )


def solution(mesh):
    placed = (
        P("fsdp", "tp", None, None),
        P("fsdp", "tp", None, None),
        P(),
        P("fsdp", None),
        P(None, "fsdp", "tp"),
        P(None, "tp"),
        P("tp", "fsdp"),
        P(),
        P(),
        P(),
        P(),
        P(),
        P("tp", "fsdp"),
        P("tp"),
        P("tp", "fsdp"),
        P(),
    )
    return jax.shard_map(
        local,
        mesh=mesh,
        in_specs=placed,
        out_specs=(
            P("fsdp", "tp", None, None),
            P("fsdp", "tp", None, None),
            P(None, "fsdp", "tp"),
            P(),
            P("tp", "fsdp"),
            P(),
            P(),
            P(),
            P(),
            P(),
            P("tp", "fsdp"),
            P(),
            P("tp", "fsdp"),
            P(),
        ),
        check_vma=False,
    )
```
